32 devices in a mesh: day: 2 (over y), chan: 4 (over z), tf: 4 (over x, core).
Axes of the slice: x: 2, y: 2, z: 4, core: 2. Of those that a mesh axis runs over, the one named last changes fastest.
Arguments:
- samples: bfloat16 [176, 512, 1024], P(('day', 'tf'), None, 'chan'), parts along dimension 0, may hold values from -6 to 6
- quality: int32 [176], P('day'), parts along dimension 0, may hold values from 0 to 3
- substack: int32 [176], P('day'), parts along dimension 0, may hold values from 0 to 1
- sources: int32 [256], replicated, may hold values from 0 to 1023, as said below
Outputs:
- stacks: bfloat16 [96, 4, 2, 256, 1024], P('tf', 'day', None, None, 'chan'), parts along dimension 1
The draws below stay inside these ranges and needn't reach their ends.
There are 2 independent parts, one for each index of `day`. The reference program is written for one: setup_inputs(seed, part) draws one part's arguments, and reference() takes and returns one part's arrays. A program takes and returns all parts, laid end to end along the dimension named above; an argument that names none is the same for every part. Nothing has to cross between parts.
Inputs may be any that keep to these rules, and one draw needn't show every extreme that they name: `sources`: virtual source s is a channel of block s // 64: its index lies in [(s // 64) * 256, (s // 64 + 1) * 256).
All inputs are finite; a program needn't handle non-finite values.
Results may differ from the reference program's by a relative error of at most 0.0084.
Values may be sent and summed in bfloat16 or wider, within the bound.
No kernel may reach another device: no remote copies, remote signals or barrier semaphores. Data moves between devices by JAX's collectives and lax.ppermute only.
A program may use at most 64 MiB of HBM per device.

```python
import math
import jax
import jax.numpy as jnp
from jax import lax

C_DEV = 256
L = 512
F = 96
K0 = 8
S = 256
G = 2
CHANNELS = 1024
W = 88
SRC_DEV = 64


def draw_sources(key, part):
    blocks = jnp.arange(S, dtype=jnp.int32) // SRC_DEV
    offsets = jax.random.randint(key, (S,), 0, C_DEV, dtype=jnp.int32)
    offsets = offsets.at[0].set(0)
    offsets = offsets.at[S - 1].set(C_DEV - 1)
    return (blocks * C_DEV + offsets).astype(jnp.int32)


def touch_ends(entries, rng, least, high):
    index_at = [jax.random.randint(jax.random.fold_in(rng, axis), (), 0, length) for axis, length in enumerate(entries.shape)]
    widest = entries.shape.index(max(entries.shape))
    neighbour = index_at[:widest] + [(index_at[widest] + 1) % entries.shape[widest]] + index_at[widest + 1:]
    return entries.at[tuple(index_at)].set(least).at[tuple(neighbour)].set(high)


def shard_levels(own_key, extent, split, low, high):
    level = 1.0
    for axis_at, shards_of in split:
        heights = jax.random.uniform(jax.random.fold_in(jax.random.fold_in(own_key, 6), axis_at), (shards_of,), jnp.float32, low / len(split), high / len(split))
        level = level * jnp.repeat(jnp.exp(heights), extent[axis_at] // shards_of).reshape((-1,) + (1,) * (len(extent) - 1 - axis_at))
    return level


def scatter_about(rng, dims, scale, limit, pieces=(), kind=jnp.bfloat16):
    values = scale * jax.random.normal(rng, dims, jnp.float32)
    if pieces:
        values = values * shard_levels(rng, dims, pieces, -0.22, 0.18)
    return jnp.clip(values, -limit, limit).astype(kind)


def setup_inputs(seed: int = 0, part: int = 0) -> dict:
    streams_of = jax.random.split(jax.random.key(seed), 5)
    part_keys = jax.random.split(jax.random.fold_in(streams_of[4], part), 5)
    samples = scatter_about(part_keys[0], (W, L, CHANNELS), 1.0, 6.0, ((0, 4), (2, 4)))
    quality = touch_ends(jax.random.randint(part_keys[1], (W,), 0, 4), jax.random.fold_in(part_keys[1], 1), 0, 3).astype(jnp.int32)
    substack = touch_ends(jax.random.randint(part_keys[2], (W,), 0, G), jax.random.fold_in(part_keys[2], 1), 0, G - 1).astype(jnp.int32)
    sources = draw_sources(jax.random.fold_in(streams_of[4], 71), part)
    return dict(samples=samples, quality=quality, substack=substack, sources=sources)


def make_table():
    freqs = K0 + jnp.arange(F, dtype=jnp.int32)
    times = jnp.arange(L, dtype=jnp.int32)
    phase = freqs[:, None] * times[None, :] % L
    angle = phase.astype(jnp.float32) * (2.0 * math.pi / L)
    scale = 1.0 / math.sqrt(L)
    table = jnp.stack([jnp.cos(angle) * scale, -jnp.sin(angle) * scale], axis=1)
    return table.astype(jnp.bfloat16)

def reference(samples, quality, substack, sources):
    table = make_table().reshape(2 * F, L)

    def one_window(window):
        values = window.astype(jnp.float32)
        power = lax.optimization_barrier(jnp.mean(values * values, axis=0, keepdims=True))
        normed = (values / jnp.sqrt(power + 1e-06)).astype(jnp.bfloat16)
        return jnp.dot(table, normed, preferred_element_type=jnp.float32).astype(jnp.bfloat16)
    spectra = lax.map(one_window, samples).reshape(W, F, 2, CHANNELS)
    groups = jnp.arange(G, dtype=jnp.int32)
    coef = jnp.where(substack[None, :] == groups[:, None], (quality[None, :].astype(jnp.float32) + 1.0) / 4.0, 0.0)
    inv_count = 1.0 / math.sqrt(W)

    def one_bin(bin_spec):
        received = jnp.transpose(bin_spec, (1, 0, 2))
        chosen = jnp.take(received, sources, axis=2).astype(jnp.float32)
        real_part = coef[:, None, :] * jnp.transpose(chosen[0])[None]
        imag_part = coef[:, None, :] * jnp.transpose(chosen[1])[None]
        real_part = real_part.astype(jnp.bfloat16).astype(jnp.float32)
        imag_part = imag_part.astype(jnp.bfloat16).astype(jnp.float32)
        first = jnp.concatenate([real_part, imag_part], axis=-1)
        second = jnp.concatenate([-imag_part, real_part], axis=-1)
        matrix = jnp.stack([first, second], axis=1).astype(jnp.bfloat16)
        summed = jnp.dot(matrix.reshape(G * 2 * S, 2 * W), received.reshape(2 * W, CHANNELS), preferred_element_type=jnp.float32)
        return (summed * inv_count).astype(jnp.bfloat16).reshape(G, 2, S, CHANNELS)
    return lax.map(one_bin, jnp.moveaxis(spectra, 1, 0))
```

```python
import math

import jax
import jax.numpy as jnp
import numpy as np
import ml_dtypes
from jax import lax
from jax.experimental import pallas as pl
from jax.experimental.pallas import tpu as pltpu
from jax.sharding import PartitionSpec as P

F = 96
K0 = 8
G = 2
CHUNKS = 3
STEP = 2
f32 = jnp.float32
bf16 = jnp.bfloat16


def make_table(length):
    freqs = K0 + np.arange(F)
    phase = freqs[:, None] * np.arange(length)[None, :] % length
    angle = phase.astype(np.float32) * np.float32(2.0 * math.pi / length)
    scale = np.float32(1.0 / math.sqrt(length))
    table = np.stack([np.cos(angle) * scale, -np.sin(angle) * scale], axis=1)
    return table.astype(np.float32).astype(ml_dtypes.bfloat16)


def make_shuffle():
    shuffle = np.zeros((128, 128), np.float32)
    for w in range(8):
        for r in range(16):
            shuffle[r * 8 + w, w * 16 + r] = 1.0
    return shuffle.astype(ml_dtypes.bfloat16)


def up(n, m):
    return -(-n // m) * m


def head_kernel(cfg, order, samples, table, shuffle, *refs):
    win, wpad, n_tf, bins, chunks = cfg
    outs, (tscr, spec) = refs[:-2], refs[-2:]
    step = pl.program_id(0)

    @pl.when(step == 0)
    def _():
        rows = [table[order[k]].astype(f32) for k in range(n_tf)]
        tscr[...] = jnp.concatenate(rows, axis=0).astype(bf16)
        for w in range(win, wpad):
            spec[w] = jnp.zeros(spec.shape[1:], bf16)

    for i in range(STEP):
        x = samples[i]
        xf = x.astype(f32)
        power = jnp.mean(xf * xf, axis=0, keepdims=True)
        y = jnp.dot(tscr[...], x, preferred_element_type=f32)
        spec[step * STEP + i] = (y * lax.rsqrt(power + 1e-06)).astype(bf16)

    @pl.when(step == pl.num_programs(0) - 1)
    def _():
        per = bins // chunks
        for grp in range(2 * F // 16):
            parts = []
            for wg in range(wpad // 8):
                block = spec[8 * wg : 8 * wg + 8, 16 * grp : 16 * grp + 16, :]
                block = block.reshape(128, block.shape[-1])
                parts.append(jnp.dot(shuffle[...], block, preferred_element_type=f32))
            for j in range(8):
                flat = grp * 8 + j
                k, f = flat // bins, flat % bins
                pieces = []
                for r in range(2):
                    row = (2 * j + r) * 8
                    pieces += [p[row : row + 8] for p in parts]
                value = jnp.concatenate(pieces, axis=0).astype(bf16)
                if k < 2:
                    outs[k][f] = value
                else:
                    outs[2 + (k - 2) * chunks + f // per][f % per] = value


def select_kernel(wpad, cols, *refs):
    slabs, out = refs[:-1], refs[-1]
    bins, rows, chans = slabs[0].shape
    lanes = cols.shape[1]
    pick = (lax.broadcasted_iota(jnp.int32, (chans, lanes), 0) == cols[...]).astype(f32).astype(bf16)
    real = lax.broadcasted_iota(jnp.int32, (wpad, lanes), 1) < lanes // 2
    for d, slab in enumerate(slabs):
        def body(p, _, d=d, slab=slab):
            flat = slab[pl.ds(2 * p, 2)].reshape(2 * rows, chans)
            got = jnp.dot(flat, pick, preferred_element_type=f32)
            both = []
            for j in range(2):
                base = j * rows
                both.append(jnp.where(real, got[base : base + wpad], got[base + wpad : base + rows]))
            out[d, p] = jnp.concatenate(both, axis=0).astype(bf16)
            return 0

        lax.fori_loop(0, bins // 2, body, 0, unroll=True)


def cross_kernel(cfg, blk, coef, eye, *refs):
    wpad, kpad, scale, n_slab, counts = cfg
    out = refs[-1]
    slabs, rest = refs[:n_slab], refs[n_slab:]
    panels = []
    for near, far in counts:
        panels.append((rest[:near], rest[near : near + far]))
        rest = rest[near + far :]
    n_blk = len(panels)
    lanes = panels[0][0][0].shape[-1]
    src = lanes // 2
    chans = slabs[0].shape[-1]
    used = wpad * n_slab

    def merged(group):
        value = group[0][...].astype(f32)
        for other in group[1:]:
            value = value + other[...].astype(f32)
        return value

    loaded = [[merged(near), merged(far)] for near, far in panels]
    for j in range(2):
        re, im = [], []
        for slab in slabs:
            v = slab[j].astype(f32)
            re.append(v[:wpad])
            im.append(v[wpad:])
        if kpad > used:
            pad = [jnp.zeros((kpad - used, chans), f32)]
            re, im = re + pad, im + pad
        re = jnp.concatenate(re, axis=0)
        im = jnp.concatenate(im, axis=0)
        right = jnp.concatenate(
            [jnp.concatenate([re, im], axis=1), jnp.concatenate([im, -re], axis=1)], axis=0
        ).astype(bf16)
        stacked = []
        for near, far in loaded:
            for value in (near, far):
                for d in range(value.shape[0]):
                    stacked.append(value[d, 0, j * wpad : (j + 1) * wpad])
            if kpad > used:
                stacked.append(jnp.zeros((kpad - used, lanes), f32))
        stacked = jnp.concatenate(stacked, axis=0).astype(bf16)
        turned = lax.dot_general(
            eye[...], stacked, (((1,), (1,)), ((), ())), preferred_element_type=f32
        )
        for g in range(G):
            weight = coef[g : g + 1, :]
            rows = []
            for b in range(n_blk):
                t = turned[:, b * kpad : (b + 1) * kpad] * weight
                rows.append(jnp.concatenate([t[:src], t[src:]], axis=1))
            left = jnp.concatenate(rows, axis=0).astype(bf16)
            got = jnp.dot(left, right, preferred_element_type=f32) * scale
            got = got.astype(bf16)
            for b in range(n_blk):
                at = pl.ds(pl.multiple_of(blk[b] * src, src), src)
                for o in range(2):
                    out[j, g, o, at, :] = got[b * src : (b + 1) * src, o * chans : (o + 1) * chans]


def shards(samples, quality, substack, sources):
    win, length, chans = samples.shape
    n_tf = lax.axis_size("tf")
    n_chan = lax.axis_size("chan")
    me = lax.axis_index("tf")
    pos = lax.axis_index("chan")
    bins = F // n_tf
    src = sources.shape[0] // n_chan
    wpad = up(win, 8)
    kpad = up(wpad * n_tf, 128)
    per = bins // CHUNKS
    rows = 2 * wpad
    order = (me ^ jnp.arange(n_tf, dtype=jnp.int32)).astype(jnp.int32)
    table = jnp.asarray(make_table(length).reshape(n_tf, 2 * bins, length))
    smem = pl.BlockSpec(memory_space=pltpu.SMEM)
    vmem = pl.BlockSpec(memory_space=pltpu.VMEM)

    shapes = [jax.ShapeDtypeStruct((bins, rows, chans), bf16)] * 2
    shapes += [jax.ShapeDtypeStruct((per, rows, chans), bf16)] * ((n_tf - 2) * CHUNKS)
    got = pl.pallas_call(
        lambda *refs: head_kernel((win, wpad, n_tf, bins, CHUNKS), *refs),
        grid=(win // STEP,),
        in_specs=[
            smem,
            pl.BlockSpec((STEP, length, chans), lambda i: (i, 0, 0)),
            pl.BlockSpec((n_tf, 2 * bins, length), lambda i: (0, 0, 0)),
            pl.BlockSpec((128, 128), lambda i: (0, 0)),
        ],
        out_specs=[pl.BlockSpec(s.shape, lambda i: (0, 0, 0)) for s in shapes],
        out_shape=shapes,
        scratch_shapes=[
            pltpu.VMEM((2 * F, length), bf16),
            pltpu.VMEM((wpad, 2 * F, chans), bf16),
        ],
        compiler_params=pltpu.CompilerParams(vmem_limit_bytes=48 * 1024 * 1024),
        name="head",
    )(order, samples, table, jnp.asarray(make_shuffle()))
    own, for_core = got[0], got[1]

    def across(value, k):
        return lax.ppermute(value, "tf", [(i, i ^ k) for i in range(n_tf)])

    core = across(for_core, 1)
    far = [
        [across(got[2 + (k - 2) * CHUNKS + q], k) for k in range(2, n_tf)] for q in range(CHUNKS)
    ]

    mine = lax.dynamic_slice_in_dim(sources, pos * src, src, 0) - pos * chans
    cols = jnp.concatenate([mine, mine])[None, :]

    def select(slabs):
        count = slabs[0].shape[0]
        return pl.pallas_call(
            lambda *refs: select_kernel(wpad, *refs),
            in_specs=[vmem] * (1 + len(slabs)),
            out_specs=vmem,
            out_shape=jax.ShapeDtypeStruct((len(slabs), count // 2, 2 * wpad, 2 * src), bf16),
            compiler_params=pltpu.CompilerParams(vmem_limit_bytes=32 * 1024 * 1024),
            name="select",
        )(cols, *slabs)

    def spread(panel):
        if n_chan == 4:
            one = lax.ppermute(panel, "chan", [(i, i ^ 1) for i in range(4)])
            two = lax.ppermute(panel, "chan", [(i, i ^ 2) for i in range(4)])
            mid = lax.ppermute(panel, "chan", [(1, 2), (2, 1)])
            end = lax.ppermute(two, "chan", [(2, 3), (1, 0)])
            return [[panel], [one], [two], [mid, end]]
        return [[panel]] + [
            [lax.ppermute(panel, "chan", [(i, (i + k) % n_chan) for i in range(n_chan)])]
            for k in range(1, n_chan)
        ]

    if n_chan == 4:
        blk = pos ^ jnp.arange(4, dtype=jnp.int32)
    else:
        blk = (pos - jnp.arange(n_chan, dtype=jnp.int32)) % n_chan
    blk = blk.astype(jnp.int32)

    coef = jnp.where(
        substack[None, :] == jnp.arange(G, dtype=jnp.int32)[:, None],
        (quality[None, :].astype(f32) + 1.0) / 4.0,
        0.0,
    ).reshape(G, n_tf, win)
    coef = jnp.pad(coef, ((0, 0), (0, 0), (0, wpad - win)))
    coef = jnp.take(coef, order, axis=1).reshape(G, n_tf * wpad)
    coef = jnp.pad(coef, ((0, 0), (0, kpad - n_tf * wpad)))
    eye = jnp.asarray(np.eye(2 * src, dtype=np.float32).astype(ml_dtypes.bfloat16))
    scale = 1.0 / math.sqrt(win * n_tf)

    near = spread(select([own, core]))
    stacks = None
    out_shape = jax.ShapeDtypeStruct((bins, G, 2, src * n_chan, chans), bf16)
    for q in range(CHUNKS):
        away = spread(select(far[q]))
        pairs = per // 2
        lead = q * pairs
        slab_all = pl.BlockSpec((2, rows, chans), lambda i, lead=lead: (lead + i, 0, 0))
        slab_one = pl.BlockSpec((2, rows, chans), lambda i: (i, 0, 0))
        args, specs, counts = [own, core] + far[q], [slab_all] * 2 + [slab_one] * (n_tf - 2), []
        for a, b in zip(near, away):
            args += a + b
            specs += [
                pl.BlockSpec((2, 1, 2 * wpad, 2 * src), lambda i, lead=lead: (0, lead + i, 0, 0))
            ] * len(a)
            specs += [
                pl.BlockSpec((n_tf - 2, 1, 2 * wpad, 2 * src), lambda i: (0, i, 0, 0))
            ] * len(b)
            counts.append((len(a), len(b)))
        cfg = (wpad, kpad, scale, n_tf, counts)
        first = stacks is None
        extra = [] if first else [stacks]

        def body(*refs, cfg=cfg, first=first):
            refs = refs if first else refs[:-2] + refs[-1:]
            cross_kernel(cfg, *refs)

        stacks = pl.pallas_call(
            body,
            grid=(pairs,),
            in_specs=[smem, pl.BlockSpec(coef.shape, lambda i: (0, 0)), pl.BlockSpec(eye.shape, lambda i: (0, 0))]
            + specs
            + [pl.BlockSpec(memory_space=pl.ANY)] * len(extra),
            out_specs=pl.BlockSpec(
                (2, G, 2, src * n_chan, chans), lambda i, lead=lead: (lead + i, 0, 0, 0, 0)
            ),
            out_shape=out_shape,
            input_output_aliases={} if first else {3 + len(args): 0},
            compiler_params=pltpu.CompilerParams(vmem_limit_bytes=32 * 1024 * 1024),
            name="cross",
        )(blk, coef, eye, *args, *extra)
    return stacks


def solution(mesh):
    in_specs = (P(("day", "tf"), None, "chan"), P("day"), P("day"), P())
    out_specs = P("tf", "day", None, None, "chan")
    return jax.shard_map(shards, mesh=mesh, in_specs=in_specs, out_specs=out_specs, check_vma=False)
```

```python
import math

import jax
import jax.numpy as jnp
import numpy as np
import ml_dtypes
from jax import lax
from jax.experimental import pallas as pl
from jax.experimental.pallas import tpu as pltpu
from jax.sharding import PartitionSpec as P

F = 96
K0 = 8
G = 2
PARTS = (2, 1)
f32 = jnp.float32
bf16 = jnp.bfloat16


def make_table(length):
    freqs = K0 + np.arange(F)
    phase = freqs[:, None] * np.arange(length)[None, :] % length
    angle = phase.astype(np.float32) * np.float32(2.0 * math.pi / length)
    scale = np.float32(1.0 / math.sqrt(length))
    table = np.stack([np.cos(angle) * scale, -np.sin(angle) * scale], axis=1)
    return table.astype(np.float32).astype(ml_dtypes.bfloat16)


def up(n, m):
    return -(-n // m) * m


def chunk_sizes(bins):
    sizes = [bins * part // sum(PARTS) for part in PARTS]
    return sizes[:-1] + [bins - sum(sizes[:-1])]


def head_kernel(cfg, order, samples_hbm, table_hbm, *refs):
    win, wpad, n_tf, bins, sizes = cfg
    outs, (samples, table, tscr, spec, sem) = refs[:-5], refs[-5:]
    copies = [
        pltpu.make_async_copy(table_hbm, table, sem.at[0]),
        pltpu.make_async_copy(samples_hbm, samples, sem.at[1]),
    ]
    for copy in copies:
        copy.start()
    to = lax.broadcasted_iota(jnp.int32, (128, 128), 0)
    at = lax.broadcasted_iota(jnp.int32, (128, 128), 1)
    shuffle = ((to % 8 == at // 16) & (to // 8 == at % 16)).astype(f32).astype(bf16)
    for w in range(win, wpad):
        spec[w] = jnp.zeros(spec.shape[1:], bf16)
    copies[0].wait()
    rows = [table[order[k]].astype(f32) for k in range(n_tf)]
    tscr[...] = jnp.concatenate(rows, axis=0).astype(bf16)
    copies[1].wait()
    for w in range(win):
        x = samples[w]
        xf = x.astype(f32)
        power = jnp.mean(xf * xf, axis=0, keepdims=True)
        y = jnp.dot(tscr[...], x, preferred_element_type=f32)
        spec[w] = (y * lax.rsqrt(power + 1e-06)).astype(bf16)
    for grp in range(2 * F // 16):
        parts = []
        for wg in range(wpad // 8):
            block = spec[8 * wg : 8 * wg + 8, 16 * grp : 16 * grp + 16, :]
            block = block.reshape(128, block.shape[-1])
            parts.append(jnp.dot(shuffle, block, preferred_element_type=f32))
        for j in range(8):
            flat = grp * 8 + j
            k, f = flat // bins, flat % bins
            pieces = []
            for r in range(2):
                row = (2 * j + r) * 8
                pieces += [p[row : row + 8] for p in parts]
            value = jnp.concatenate(pieces, axis=0).astype(bf16)
            if k < 2:
                outs[k][f] = value
            else:
                q = 0
                while f >= sizes[q]:
                    f, q = f - sizes[q], q + 1
                outs[2 + (k - 2) * len(sizes) + q][f] = value


def select_kernel(wpad, cols, *refs):
    slabs, out = refs[:-1], refs[-1]
    bins, rows, chans = slabs[0].shape
    lanes = cols.shape[1]
    pick = (lax.broadcasted_iota(jnp.int32, (chans, lanes), 0) == cols[...]).astype(f32).astype(bf16)
    real = lax.broadcasted_iota(jnp.int32, (wpad, lanes), 1) < lanes // 2
    for d, slab in enumerate(slabs):
        def body(p, _, d=d, slab=slab):
            flat = slab[pl.ds(2 * p, 2)].reshape(2 * rows, chans)
            got = jnp.dot(flat, pick, preferred_element_type=f32)
            both = []
            for j in range(2):
                base = j * rows
                both.append(jnp.where(real, got[base : base + wpad], got[base + wpad : base + rows]))
            out[d, p] = jnp.concatenate(both, axis=0).astype(bf16)
            return 0

        lax.fori_loop(0, bins // 2, body, 0, unroll=True)


def cross_kernel(cfg, blk, coef, eye, *refs):
    wpad, kpad, scale, n_slab, counts, lead = cfg
    out, buf, sem = refs[-3:]
    slabs, rest = refs[:n_slab], refs[n_slab:-3]
    panels = []
    for near, far in counts:
        panels.append((rest[:near], rest[near : near + far]))
        rest = rest[near + far :]
    n_blk = len(panels)
    lanes = panels[0][0][0].shape[-1]
    src = lanes // 2
    chans = slabs[0].shape[-1]
    used = wpad * n_slab
    pairs = buf.shape[0]

    def copy_out(p, b):
        at = pl.ds(pl.multiple_of(blk[b] * src, src), src)
        return pltpu.make_async_copy(
            buf.at[p, :, :, :, pl.ds(b * src, src), :],
            out.at[pl.ds(2 * (lead + p), 2), :, :, at, :],
            sem.at[p, b],
        )

    def loaded(group, d, at):
        value = group[0][d, at].astype(f32)
        for other in group[1:]:
            value = value + other[d, at].astype(f32)
        return value

    def pair(p, _):
        stacks = [[], []]
        for near, far in panels:
            for group, at in ((near, lead + p), (far, p)):
                for d in range(group[0].shape[0]):
                    value = loaded(group, d, at)
                    for j in range(2):
                        stacks[j].append(value[j * wpad : (j + 1) * wpad])
            if kpad > used:
                for j in range(2):
                    stacks[j].append(jnp.zeros((kpad - used, lanes), f32))
        for j in range(2):
            re, im = [], []
            for i, slab in enumerate(slabs):
                v = slab[2 * ((lead if i < 2 else 0) + p) + j].astype(f32)
                re.append(v[:wpad])
                im.append(v[wpad:])
            if kpad > used:
                pad = [jnp.zeros((kpad - used, chans), f32)]
                re, im = re + pad, im + pad
            re = jnp.concatenate(re, axis=0)
            im = jnp.concatenate(im, axis=0)
            right = jnp.concatenate(
                [jnp.concatenate([re, im], axis=1), jnp.concatenate([im, -re], axis=1)], axis=0
            ).astype(bf16)
            stacked = jnp.concatenate(stacks[j], axis=0).astype(bf16)
            turned = lax.dot_general(
                eye[...], stacked, (((1,), (1,)), ((), ())), preferred_element_type=f32
            )
            rows = []
            for g in range(G):
                weight = coef[g : g + 1, :]
                for b in range(n_blk):
                    t = turned[:, b * kpad : (b + 1) * kpad] * weight
                    rows.append(jnp.concatenate([t[:src], t[src:]], axis=1))
            left = jnp.concatenate(rows, axis=0).astype(bf16)
            got = (jnp.dot(left, right, preferred_element_type=f32) * scale).astype(bf16)
            tall = n_blk * src
            for g in range(G):
                for o in range(2):
                    buf[p, j, g, o] = got[g * tall : (g + 1) * tall, o * chans : (o + 1) * chans]
        for b in range(n_blk):
            copy_out(p, b).start()
        return 0

    lax.fori_loop(0, pairs, pair, 0)
    for p in range(pairs):
        for b in range(n_blk):
            copy_out(p, b).wait()


def shards(samples, quality, substack, sources):
    win, length, chans = samples.shape
    n_tf = lax.axis_size("tf")
    n_chan = lax.axis_size("chan")
    me = lax.axis_index("tf")
    pos = lax.axis_index("chan")
    bins = F // n_tf
    src = sources.shape[0] // n_chan
    wpad = up(win, 8)
    kpad = up(wpad * n_tf, 128)
    sizes = chunk_sizes(bins)
    chunks = len(sizes)
    rows = 2 * wpad
    order = (me ^ jnp.arange(n_tf, dtype=jnp.int32)).astype(jnp.int32)
    table = jnp.asarray(make_table(length).reshape(n_tf, 2 * bins, length))
    smem = pl.BlockSpec(memory_space=pltpu.SMEM)
    vmem = pl.BlockSpec(memory_space=pltpu.VMEM)
    hbm = pl.BlockSpec(memory_space=pltpu.HBM)

    shapes = [jax.ShapeDtypeStruct((bins, rows, chans), bf16)] * 2
    for _ in range(n_tf - 2):
        shapes += [jax.ShapeDtypeStruct((size, rows, chans), bf16) for size in sizes]
    got = pl.pallas_call(
        lambda *refs: head_kernel((win, wpad, n_tf, bins, sizes), *refs),
        in_specs=[smem, hbm, hbm],
        out_specs=[vmem] * len(shapes),
        out_shape=shapes,
        scratch_shapes=[
            pltpu.VMEM(samples.shape, bf16),
            pltpu.VMEM(table.shape, bf16),
            pltpu.VMEM((2 * F, length), bf16),
            pltpu.VMEM((wpad, 2 * F, chans), bf16),
            pltpu.SemaphoreType.DMA((2,)),
        ],
        compiler_params=pltpu.CompilerParams(vmem_limit_bytes=20 * 1024 * 1024),
        name="head",
    )(order, samples, table)
    own, for_core = got[0], got[1]

    def across(value, k):
        return lax.ppermute(value, "tf", [(i, i ^ k) for i in range(n_tf)])

    core = across(for_core, 1)
    far = [
        [across(got[2 + (k - 2) * chunks + q], k) for k in range(2, n_tf)] for q in range(chunks)
    ]

    mine = lax.dynamic_slice_in_dim(sources, pos * src, src, 0) - pos * chans
    cols = jnp.concatenate([mine, mine])[None, :]

    def select(slabs):
        count = slabs[0].shape[0]
        return pl.pallas_call(
            lambda *refs: select_kernel(wpad, *refs),
            in_specs=[vmem] * (1 + len(slabs)),
            out_specs=vmem,
            out_shape=jax.ShapeDtypeStruct((len(slabs), count // 2, 2 * wpad, 2 * src), bf16),
            compiler_params=pltpu.CompilerParams(vmem_limit_bytes=12 * 1024 * 1024),
            name="select",
        )(cols, *slabs)

    def spread(panel):
        if n_chan == 4:
            one = lax.ppermute(panel, "chan", [(i, i ^ 1) for i in range(4)])
            two = lax.ppermute(panel, "chan", [(i, i ^ 2) for i in range(4)])
            mid = lax.ppermute(panel, "chan", [(1, 2), (2, 1)])
            end = lax.ppermute(two, "chan", [(2, 3), (1, 0)])
            return [[panel], [one], [two], [mid, end]]
        return [[panel]] + [
            [lax.ppermute(panel, "chan", [(i, (i + k) % n_chan) for i in range(n_chan)])]
            for k in range(1, n_chan)
        ]

    if n_chan == 4:
        blk = pos ^ jnp.arange(4, dtype=jnp.int32)
    else:
        blk = (pos - jnp.arange(n_chan, dtype=jnp.int32)) % n_chan
    blk = blk.astype(jnp.int32)

    coef = jnp.where(
        substack[None, :] == jnp.arange(G, dtype=jnp.int32)[:, None],
        (quality[None, :].astype(f32) + 1.0) / 4.0,
        0.0,
    ).reshape(G, n_tf, win)
    coef = jnp.pad(coef, ((0, 0), (0, 0), (0, wpad - win)))
    coef = jnp.take(coef, order, axis=1).reshape(G, n_tf * wpad)
    coef = jnp.pad(coef, ((0, 0), (0, kpad - n_tf * wpad)))
    eye = jnp.asarray(np.eye(2 * src, dtype=np.float32).astype(ml_dtypes.bfloat16))
    scale = 1.0 / math.sqrt(win * n_tf)

    near = spread(select([own, core]))
    away = [spread(select(far[q])) for q in range(chunks)]
    out_shape = jax.ShapeDtypeStruct((bins, G, 2, src * n_chan, chans), bf16)
    groups = [[0, 1, 2], [3]] if n_chan == 4 else [list(range(n_chan))]
    stacks = None
    for q, size in enumerate(sizes):
        for group in groups:
            pairs = size // 2
            args, counts = [own, core] + far[q], []
            for b in group:
                args += near[b] + away[q][b]
                counts.append((len(near[b]), len(away[q][b])))
            cfg = (wpad, kpad, scale, n_tf, counts, sum(sizes[:q]) // 2)
            first = stacks is None
            extra = [] if first else [stacks]

            def body(*refs, cfg=cfg, first=first):
                cross_kernel(cfg, *(refs if first else refs[:-4] + refs[-3:]))

            stacks = pl.pallas_call(
                body,
                in_specs=[smem] + [vmem] * (2 + len(args)) + [hbm] * len(extra),
                out_specs=hbm,
                out_shape=out_shape,
                scratch_shapes=[
                    pltpu.VMEM((pairs, 2, G, 2, len(group) * src, chans), bf16),
                    pltpu.SemaphoreType.DMA((pairs, len(group))),
                ],
                input_output_aliases={} if first else {3 + len(args): 0},
                compiler_params=pltpu.CompilerParams(vmem_limit_bytes=20 * 1024 * 1024),
                name="cross",
            )(blk[np.array(group)], coef, eye, *args, *extra)
    return stacks


def solution(mesh):
    in_specs = (P(("day", "tf"), None, "chan"), P("day"), P("day"), P())
    out_specs = P("tf", "day", None, None, "chan")
    return jax.shard_map(shards, mesh=mesh, in_specs=in_specs, out_specs=out_specs, check_vma=False)
```

```python
import math

import jax
import jax.numpy as jnp
import numpy as np
import ml_dtypes
from jax import lax
from jax.experimental import pallas as pl
from jax.experimental.pallas import tpu as pltpu
from jax.sharding import PartitionSpec as P

F = 96
K0 = 8
G = 2
PARTS = (2, 1)
f32 = jnp.float32
bf16 = jnp.bfloat16


def make_table(length):
    freqs = K0 + np.arange(F)
    phase = freqs[:, None] * np.arange(length)[None, :] % length
    angle = phase.astype(np.float32) * np.float32(2.0 * math.pi / length)
    scale = np.float32(1.0 / math.sqrt(length))
    table = np.stack([np.cos(angle) * scale, -np.sin(angle) * scale], axis=1)
    return table.astype(np.float32).astype(ml_dtypes.bfloat16)


def up(n, m):
    return -(-n // m) * m


def chunk_sizes(bins):
    sizes = [bins * part // sum(PARTS) for part in PARTS]
    return sizes[:-1] + [bins - sum(sizes[:-1])]


def head_kernel(cfg, order, samples_hbm, table_hbm, *refs):
    win, wpad, n_tf, bins, sizes = cfg
    outs, (samples, table, tscr, spec, buf, sem) = refs[:-6], refs[-6:]
    load_table = pltpu.make_async_copy(table_hbm, table, sem.at[0])
    load_samples = pltpu.make_async_copy(samples_hbm, samples, sem.at[1])
    load_table.start()
    load_samples.start()
    to = lax.broadcasted_iota(jnp.int32, (128, 128), 0)
    at = lax.broadcasted_iota(jnp.int32, (128, 128), 1)
    shuffle = ((to % 8 == at // 16) & (to // 8 == at % 16)).astype(f32).astype(bf16)
    for w in range(win, wpad):
        spec[w] = jnp.zeros(spec.shape[1:], bf16)
    load_table.wait()
    rows = [table[order[k]].astype(f32) for k in range(n_tf)]
    tscr[...] = jnp.concatenate(rows, axis=0).astype(bf16)
    load_samples.wait()
    for w in range(win):
        x = samples[w]
        xf = x.astype(f32)
        power = jnp.mean(xf * xf, axis=0, keepdims=True)
        y = jnp.dot(tscr[...], x, preferred_element_type=f32)
        spec[w] = (y * lax.rsqrt(power + 1e-06)).astype(bf16)
    spans = [(0, bins), (bins, bins)]
    for k in range(2, n_tf):
        base = k * bins
        for size in sizes:
            spans.append((base, size))
            base += size
    stores = [
        pltpu.make_async_copy(buf.at[pl.ds(base, size)], out, sem.at[2 + i])
        for i, ((base, size), out) in enumerate(zip(spans, outs))
    ]
    done = set()
    for grp in reversed(range(2 * F // 16)):
        parts = []
        for wg in range(wpad // 8):
            block = spec[8 * wg : 8 * wg + 8, 16 * grp : 16 * grp + 16, :]
            block = block.reshape(128, block.shape[-1])
            parts.append(jnp.dot(shuffle, block, preferred_element_type=f32))
        for j in range(8):
            pieces = []
            for r in range(2):
                row = (2 * j + r) * 8
                pieces += [p[row : row + 8] for p in parts]
            buf[grp * 8 + j] = jnp.concatenate(pieces, axis=0).astype(bf16)
        for i, (base, _) in enumerate(spans):
            if base >= grp * 8 and i not in done:
                done.add(i)
                stores[i].start()
    for store in stores:
        store.wait()


def select_kernel(cols, *refs):
    slabs, out = refs[:-1], refs[-1]
    bins, rows, chans = slabs[0].shape
    lanes = cols.shape[1]
    pick = (lax.broadcasted_iota(jnp.int32, (chans, lanes), 0) == cols[...]).astype(f32).astype(bf16)
    first = lax.broadcasted_iota(jnp.int32, (rows, lanes), 1) < lanes // 2
    for d, slab in enumerate(slabs):
        for p in range(bins // 2):
            flat = slab[2 * p : 2 * p + 2].reshape(2 * rows, chans)
            got = jnp.dot(flat, pick, preferred_element_type=f32)
            out[d, p] = jnp.where(first, got[:rows], got[rows:]).astype(bf16)


def cross_kernel(cfg, blk, coef, *refs):
    wpad, scale, n_slab, counts, lead = cfg
    out, buf, sem = refs[-3:]
    slabs, rest = refs[:n_slab], refs[n_slab:-3]
    panels = []
    for near, far in counts:
        panels.append((rest[:near], rest[near : near + far]))
        rest = rest[near + far :]
    n_blk = len(panels)
    src = panels[0][0][0].shape[-1] // 2
    chans = slabs[0].shape[-1]
    tall = n_blk * src
    pairs = buf.shape[0]

    def copy_out(p, b):
        at = pl.ds(pl.multiple_of(blk[b] * src, src), src)
        return pltpu.make_async_copy(
            buf.at[p, :, :, :, pl.ds(b * src, src), :],
            out.at[pl.ds(2 * (lead + p), 2), :, :, at, :],
            sem.at[p, b],
        )

    def pair(p, _):
        turned = []
        for near, far in panels:
            stack = []
            for group, at in ((near, lead + p), (far, p)):
                for d in range(group[0].shape[0]):
                    value = group[0][d, at].astype(f32)
                    for other in group[1:]:
                        value = value + other[d, at].astype(f32)
                    stack.append(value)
            turned.append(jnp.transpose(jnp.concatenate(stack, axis=0)))
        for j in range(2):
            plain, swapped = [], []
            for i, slab in enumerate(slabs):
                v = slab[2 * ((lead if i < 2 else 0) + p) + j]
                plain.append(v)
                v = v.astype(f32)
                swapped += [v[wpad:], -v[:wpad]]
            plain = jnp.concatenate(plain, axis=0)
            swapped = jnp.concatenate(swapped, axis=0).astype(bf16)
            right = jnp.concatenate([plain, swapped], axis=1)
            left = [
                (t[src * j : src * (j + 1)] * coef[g : g + 1]).astype(bf16)
                for g in range(G)
                for t in turned
            ]
            left = jnp.concatenate(left, axis=0)
            got = (jnp.dot(left, right, preferred_element_type=f32) * scale).astype(bf16)
            for g in range(G):
                for o in range(2):
                    buf[p, j, g, o] = got[g * tall : (g + 1) * tall, o * chans : (o + 1) * chans]
        for b in range(n_blk):
            copy_out(p, b).start()
        return 0

    lax.fori_loop(0, pairs, pair, 0, unroll=4 if pairs % 4 == 0 else 2 if pairs % 2 == 0 else 1)
    for p in range(pairs):
        for b in range(n_blk):
            copy_out(p, b).wait()


def cost(us):
    return pl.CostEstimate(flops=int(us * 1.1e9), bytes_accessed=int(us * 3e6), transcendentals=0)


def shards(samples, quality, substack, sources):
    win, length, chans = samples.shape
    n_tf = lax.axis_size("tf")
    n_chan = lax.axis_size("chan")
    me = lax.axis_index("tf")
    pos = lax.axis_index("chan")
    bins = F // n_tf
    src = sources.shape[0] // n_chan
    wpad = up(win, 8)
    sizes = chunk_sizes(bins)
    chunks = len(sizes)
    rows = 2 * wpad
    order = (me ^ jnp.arange(n_tf, dtype=jnp.int32)).astype(jnp.int32)
    table = jnp.asarray(make_table(length).reshape(n_tf, 2 * bins, length))
    smem = pl.BlockSpec(memory_space=pltpu.SMEM)
    vmem = pl.BlockSpec(memory_space=pltpu.VMEM)
    hbm = pl.BlockSpec(memory_space=pltpu.HBM)

    shapes = [jax.ShapeDtypeStruct((bins, rows, chans), bf16)] * 2
    for _ in range(n_tf - 2):
        shapes += [jax.ShapeDtypeStruct((size, rows, chans), bf16) for size in sizes]
    got = pl.pallas_call(
        lambda *refs: head_kernel((win, wpad, n_tf, bins, sizes), *refs),
        in_specs=[smem, hbm, hbm],
        out_specs=[hbm] * len(shapes),
        out_shape=shapes,
        scratch_shapes=[
            pltpu.VMEM(samples.shape, bf16),
            pltpu.VMEM(table.shape, bf16),
            pltpu.VMEM((2 * F, length), bf16),
            pltpu.VMEM((wpad, 2 * F, chans), bf16),
            pltpu.VMEM((F, rows, chans), bf16),
            pltpu.SemaphoreType.DMA((2 + len(shapes),)),
        ],
        compiler_params=pltpu.CompilerParams(vmem_limit_bytes=57 * 1024 * 1024),
        cost_estimate=cost(5),
        name="head",
    )(order, samples, table)
    own, for_core = got[0], got[1]

    def across(value, k):
        return lax.ppermute(value, "tf", [(i, i ^ k) for i in range(n_tf)])

    core = across(for_core, 1)
    far = [
        [across(got[2 + (k - 2) * chunks + q], k) for k in range(2, n_tf)] for q in range(chunks)
    ]

    mine = lax.dynamic_slice_in_dim(sources, pos * src, src, 0) - pos * chans
    cols = jnp.concatenate([mine, mine])[None, :]

    def select(slabs):
        count = slabs[0].shape[0]
        return pl.pallas_call(
            select_kernel,
            in_specs=[vmem] * (1 + len(slabs)),
            out_specs=vmem,
            out_shape=jax.ShapeDtypeStruct((len(slabs), count // 2, rows, 2 * src), bf16),
            cost_estimate=cost(0.5),
            compiler_params=pltpu.CompilerParams(vmem_limit_bytes=12 * 1024 * 1024),
            name="select",
        )(cols, *slabs)

    def spread(panel):
        if n_chan == 4:
            two = lax.ppermute(panel, "chan", [(i, i ^ 2) for i in range(4)])
            one = lax.ppermute(panel, "chan", [(i, i ^ 1) for i in range(4)])
            later, one, two = lax.optimization_barrier((panel, one, two))
            end = lax.ppermute(two, "chan", [(2, 3), (1, 0)])
            mid = lax.ppermute(later, "chan", [(1, 2), (2, 1)])
            return [[panel], [one], [two], [mid, end]]
        return [[panel]] + [
            [lax.ppermute(panel, "chan", [(i, (i + k) % n_chan) for i in range(n_chan)])]
            for k in range(1, n_chan)
        ]

    if n_chan == 4:
        blk = pos ^ jnp.arange(4, dtype=jnp.int32)
    else:
        blk = (pos - jnp.arange(n_chan, dtype=jnp.int32)) % n_chan
    blk = blk.astype(jnp.int32)

    coef = jnp.where(
        substack[None, :] == jnp.arange(G, dtype=jnp.int32)[:, None],
        (quality[None, :].astype(f32) + 1.0) / 4.0,
        0.0,
    ).reshape(G, n_tf, win)
    coef = jnp.pad(coef, ((0, 0), (0, 0), (0, wpad - win)))
    coef = jnp.take(jnp.concatenate([coef, coef], axis=2), order, axis=1).reshape(G, n_tf * rows)
    scale = 1.0 / math.sqrt(win * n_tf)

    near = spread(select([own, core]))
    away, before = [], [near[1][0], near[2][0]]
    for q in range(chunks):
        if q:
            *far[q], _, _, _ = lax.optimization_barrier((*far[q], *before, panel))
        panel = select(far[q])
        away.append(spread(panel))
    out_shape = jax.ShapeDtypeStruct((bins, G, 2, src * n_chan, chans), bf16)
    groups = [[0, 1, 2], [3]] if n_chan == 4 else [list(range(n_chan))]
    stacks = None
    for q, size in enumerate(sizes):
        for group in groups:
            pairs = size // 2
            args, counts = [own, core] + far[q], []
            for b in group:
                args += near[b] + away[q][b]
                counts.append((len(near[b]), len(away[q][b])))
            cfg = (wpad, scale, n_tf, counts, sum(sizes[:q]) // 2)
            first = stacks is None
            extra = [] if first else [stacks]

            def body(*refs, cfg=cfg, first=first):
                cross_kernel(cfg, *(refs if first else refs[:-4] + refs[-3:]))

            stacks = pl.pallas_call(
                body,
                in_specs=[smem] + [vmem] * (1 + len(args)) + [hbm] * len(extra),
                out_specs=hbm,
                out_shape=out_shape,
                scratch_shapes=[
                    pltpu.VMEM((pairs, 2, G, 2, len(group) * src, chans), bf16),
                    pltpu.SemaphoreType.DMA((pairs, len(group))),
                ],
                input_output_aliases={} if first else {2 + len(args): 0},
                compiler_params=pltpu.CompilerParams(vmem_limit_bytes=20 * 1024 * 1024),
                cost_estimate=cost(1.5 + size * len(group) * src / 1000),
                name="cross",
            )(blk[np.array(group)], coef, *args, *extra)
    return stacks


def solution(mesh):
    in_specs = (P(("day", "tf"), None, "chan"), P("day"), P("day"), P())
    out_specs = P("tf", "day", None, None, "chan")
    return jax.shard_map(shards, mesh=mesh, in_specs=in_specs, out_specs=out_specs, check_vma=False)
```

```python
import math

import jax
import jax.numpy as jnp
from jax import lax
from jax.experimental import pallas as pl
from jax.experimental.pallas import tpu as pltpu
from jax.sharding import PartitionSpec as P

F = 96
K0 = 8
G = 2
PARTS = (1,)
f32 = jnp.float32
bf16 = jnp.bfloat16


def up(n, m):
    return -(-n // m) * m


def chunk_sizes(bins):
    sizes = [bins * part // sum(PARTS) for part in PARTS]
    return sizes[:-1] + [bins - sum(sizes[:-1])]


def head_kernel(cfg, samples_hbm, *refs):
    win, wpad, n_tf, bins, sizes = cfg
    outs, (samples, table, spec, sem) = refs[:-4], refs[-4:]
    load = pltpu.make_async_copy(samples_hbm, samples, sem)
    load.start()
    shape = table.shape
    length = shape[1]
    row = lax.broadcasted_iota(jnp.int32, (shape[0], 1), 0)
    owner = lax.axis_index("tf") ^ (row // (2 * bins))
    freq = K0 + owner * bins + (row % (2 * bins)) // 2
    phase = freq * lax.broadcasted_iota(jnp.int32, shape, 1)
    phase = (phase + (row % 2) * (length // 4)) % length
    angle = phase.astype(f32) * (2.0 * math.pi / length)
    table[...] = (jnp.cos(angle) * (1.0 / math.sqrt(length))).astype(bf16)
    to = lax.broadcasted_iota(jnp.int32, (128, 128), 0)
    at = lax.broadcasted_iota(jnp.int32, (128, 128), 1)
    shuffle = ((to % 8 == at // 16) & (to // 8 == at % 16)).astype(f32).astype(bf16)
    for w in range(win, wpad):
        spec[w] = jnp.zeros(spec.shape[1:], bf16)
    load.wait()
    for w in range(win):
        x = samples[w]
        xf = x.astype(f32)
        power = jnp.mean(xf * xf, axis=0, keepdims=True)
        y = jnp.dot(table[...], x, preferred_element_type=f32)
        spec[w] = (y * lax.rsqrt(power + 1e-06)).astype(bf16)
    for grp in range(2 * F // 16):
        parts = []
        for wg in range(wpad // 8):
            block = spec[8 * wg : 8 * wg + 8, 16 * grp : 16 * grp + 16, :]
            block = block.reshape(128, block.shape[-1])
            parts.append(jnp.dot(shuffle, block, preferred_element_type=f32))
        for j in range(8):
            flat = grp * 8 + j
            k, f = flat // bins, flat % bins
            pieces = []
            for r in range(2):
                row = (2 * j + r) * 8
                pieces += [p[row : row + 8] for p in parts]
            value = jnp.concatenate(pieces, axis=0).astype(bf16)
            if k < 2:
                outs[k][f] = value
            else:
                q = 0
                while f >= sizes[q]:
                    f, q = f - sizes[q], q + 1
                outs[2 + (k - 2) * len(sizes) + q][f] = value


def select_kernel(cols, *refs):
    slabs, out = refs[:-1], refs[-1]
    bins, rows, chans = slabs[0].shape
    lanes = cols.shape[1]
    pick = (lax.broadcasted_iota(jnp.int32, (chans, lanes), 0) == cols[...]).astype(f32).astype(bf16)
    first = lax.broadcasted_iota(jnp.int32, (rows, lanes), 1) < lanes // 2
    for d, slab in enumerate(slabs):
        for p in range(bins // 2):
            flat = slab[2 * p : 2 * p + 2].reshape(2 * rows, chans)
            got = jnp.dot(flat, pick, preferred_element_type=f32)
            out[d, p] = jnp.where(first, got[:rows], got[rows:]).astype(bf16)


def cross_kernel(cfg, coef, *refs):
    wpad, scale, n_slab, counts, lead, owners = cfg
    pos = lax.axis_index("chan")
    blk = owners(pos)
    out, buf, sem = refs[-3:]
    slabs, rest = refs[:n_slab], refs[n_slab:-3]
    panels = []
    for near, far in counts:
        panels.append((rest[:near], rest[near : near + far]))
        rest = rest[near + far :]
    n_blk = len(panels)
    src = panels[0][0][0].shape[-1] // 2
    chans = slabs[0].shape[-1]
    tall = n_blk * src
    pairs = buf.shape[0]

    def copy_out(p, b):
        at = pl.ds(pl.multiple_of(blk[b] * src, src), src)
        return pltpu.make_async_copy(
            buf.at[p, :, :, :, pl.ds(b * src, src), :],
            out.at[pl.ds(2 * (lead + p), 2), :, :, at, :],
            sem.at[p, b],
        )

    def pair(p, _):
        turned = []
        for near, far in panels:
            stack = []
            for group, at in ((near, lead + p), (far, p)):
                for d in range(group[0].shape[0]):
                    value = group[0][d, at].astype(f32)
                    for other in group[1:]:
                        value = value + other[d, at].astype(f32)
                    stack.append(value)
            turned.append(jnp.transpose(jnp.concatenate(stack, axis=0)))
        for j in range(2):
            plain, swapped = [], []
            for i, slab in enumerate(slabs):
                v = slab[2 * ((lead if i < 2 else 0) + p) + j]
                plain.append(v)
                v = v.astype(f32)
                swapped += [v[wpad:], -v[:wpad]]
            plain = jnp.concatenate(plain, axis=0)
            swapped = jnp.concatenate(swapped, axis=0).astype(bf16)
            right = jnp.concatenate([plain, swapped], axis=1)
            left = [
                (t[src * j : src * (j + 1)] * coef[g : g + 1]).astype(bf16)
                for g in range(G)
                for t in turned
            ]
            left = jnp.concatenate(left, axis=0)
            got = (jnp.dot(left, right, preferred_element_type=f32) * scale).astype(bf16)
            for g in range(G):
                for o in range(2):
                    buf[p, j, g, o] = got[g * tall : (g + 1) * tall, o * chans : (o + 1) * chans]
        for b in range(n_blk):
            copy_out(p, b).start()
        return 0

    lax.fori_loop(0, pairs, pair, 0, unroll=4 if pairs % 4 == 0 else 2 if pairs % 2 == 0 else 1)
    for p in range(pairs):
        for b in range(n_blk):
            copy_out(p, b).wait()


def cost(us):
    return pl.CostEstimate(flops=int(us * 1.1e9), bytes_accessed=int(us * 3e6), transcendentals=0)


def shards(samples, quality, substack, sources):
    win, length, chans = samples.shape
    n_tf = lax.axis_size("tf")
    n_chan = lax.axis_size("chan")
    me = lax.axis_index("tf")
    pos = lax.axis_index("chan")
    bins = F // n_tf
    src = sources.shape[0] // n_chan
    wpad = up(win, 8)
    sizes = chunk_sizes(bins)
    chunks = len(sizes)
    rows = 2 * wpad
    order = (me ^ jnp.arange(n_tf, dtype=jnp.int32)).astype(jnp.int32)
    vmem = pl.BlockSpec(memory_space=pltpu.VMEM)
    hbm = pl.BlockSpec(memory_space=pltpu.HBM)

    shapes = [jax.ShapeDtypeStruct((bins, rows, chans), bf16)] * 2
    for _ in range(n_tf - 2):
        shapes += [jax.ShapeDtypeStruct((size, rows, chans), bf16) for size in sizes]
    got = pl.pallas_call(
        lambda *refs: head_kernel((win, wpad, n_tf, bins, sizes), *refs),
        in_specs=[hbm],
        out_specs=[vmem] * len(shapes),
        out_shape=shapes,
        scratch_shapes=[
            pltpu.VMEM(samples.shape, bf16),
            pltpu.VMEM((2 * F, length), bf16),
            pltpu.VMEM((wpad, 2 * F, chans), bf16),
            pltpu.SemaphoreType.DMA,
        ],
        compiler_params=pltpu.CompilerParams(vmem_limit_bytes=50 * 1024 * 1024),
        cost_estimate=cost(5),
        name="head",
    )(samples)
    own, for_core = got[0], got[1]

    def across(value, k):
        return lax.ppermute(value, "tf", [(i, i ^ k) for i in range(n_tf)])

    core = across(for_core, 1)
    mine = lax.dynamic_slice_in_dim(sources, pos * src, src, 0) - pos * chans
    cols = jnp.concatenate([mine, mine])[None, :]

    def select(slabs):
        count = slabs[0].shape[0]
        return pl.pallas_call(
            select_kernel,
            in_specs=[vmem] * (1 + len(slabs)),
            out_specs=vmem,
            out_shape=jax.ShapeDtypeStruct((len(slabs), count // 2, rows, 2 * src), bf16),
            cost_estimate=cost(0.5),
            compiler_params=pltpu.CompilerParams(vmem_limit_bytes=12 * 1024 * 1024),
            name="select",
        )(cols, *slabs)

    def spread(panel):
        if n_chan == 4:
            two = lax.ppermute(panel, "chan", [(i, i ^ 2) for i in range(4)])
            one = lax.ppermute(panel, "chan", [(i, i ^ 1) for i in range(4)])
            later, one, two = lax.optimization_barrier((panel, one, two))
            end = lax.ppermute(two, "chan", [(2, 3), (1, 0)])
            mid = lax.ppermute(later, "chan", [(1, 2), (2, 1)])
            return [[panel], [one], [two], [mid, end]]
        return [[panel]] + [
            [lax.ppermute(panel, "chan", [(i, (i + k) % n_chan) for i in range(n_chan)])]
            for k in range(1, n_chan)
        ]

    coef = jnp.where(
        substack[None, :] == jnp.arange(G, dtype=jnp.int32)[:, None],
        (quality[None, :].astype(f32) + 1.0) / 4.0,
        0.0,
    ).reshape(G, n_tf, win)
    coef = jnp.pad(coef, ((0, 0), (0, 0), (0, wpad - win)))
    coef = jnp.take(jnp.concatenate([coef, coef], axis=2), order, axis=1).reshape(G, n_tf * rows)
    scale = 1.0 / math.sqrt(win * n_tf)

    outgoing = [[got[2 + k * chunks + q] for k in range(n_tf - 2)] for q in range(chunks)]
    panel = select([own, core])
    far, away = [], []
    for q in range(chunks):
        if q:
            *outgoing[q], panel = lax.optimization_barrier((*outgoing[q], panel))
        far.append([across(value, k + 2) for k, value in enumerate(outgoing[q])])
    near = spread(panel)
    before = near[1] + near[2]
    for q in range(chunks):
        *far[q], panel = lax.optimization_barrier((*far[q], panel, *before))[: n_tf - 1]
        panel = select(far[q])
        weights, panel = lax.optimization_barrier((coef, panel))
        away.append(spread(panel))
        before = away[q][1] + away[q][2]
    out_shape = jax.ShapeDtypeStruct((bins, G, 2, src * n_chan, chans), bf16)
    groups = [[0, 1, 2], [3]] if n_chan == 4 else [list(range(n_chan))]
    stacks = None
    for q, size in enumerate(sizes):
        for group in groups:
            pairs = size // 2
            args, counts = [own, core] + far[q], []
            for b in group:
                args += near[b] + away[q][b]
                counts.append((len(near[b]), len(away[q][b])))

            def owners(at, group=group):
                return [at ^ b if n_chan == 4 else lax.rem(at - b + n_chan, n_chan) for b in group]

            cfg = (wpad, scale, n_tf, counts, sum(sizes[:q]) // 2, owners)
            first = stacks is None
            extra = [] if first else [stacks]

            def body(*refs, cfg=cfg, first=first):
                cross_kernel(cfg, *(refs if first else refs[:-4] + refs[-3:]))

            stacks = pl.pallas_call(
                body,
                in_specs=[vmem] * (1 + len(args)) + [hbm] * len(extra),
                out_specs=hbm,
                out_shape=out_shape,
                scratch_shapes=[
                    pltpu.VMEM((pairs, 2, G, 2, len(group) * src, chans), bf16),
                    pltpu.SemaphoreType.DMA((pairs, len(group))),
                ],
                input_output_aliases={} if first else {1 + len(args): 0},
                compiler_params=pltpu.CompilerParams(vmem_limit_bytes=20 * 1024 * 1024),
                cost_estimate=cost(1.5 + size * len(group) * src / 1000),
                name="cross",
            )(weights, *args, *extra)
    return stacks


def solution(mesh):
    in_specs = (P(("day", "tf"), None, "chan"), P("day"), P("day"), P())
    out_specs = P("tf", "day", None, None, "chan")
    return jax.shard_map(shards, mesh=mesh, in_specs=in_specs, out_specs=out_specs, check_vma=False)
```

```python
import math

import jax
import jax.numpy as jnp
from jax import lax
from jax.experimental import pallas as pl
from jax.experimental.pallas import tpu as pltpu
from jax.sharding import PartitionSpec as P

F = 96
K0 = 8
G = 2
UNROLL = 3
f32 = jnp.float32
bf16 = jnp.bfloat16


def head_kernel(cfg, samples_hbm, *refs):
    win, n_tf, bins = cfg
    outs, (samples, table, spec, sem) = refs[:-4], refs[-4:]
    load = pltpu.make_async_copy(samples_hbm, samples, sem)
    load.start()
    shape = table.shape
    length = shape[1]
    row = lax.broadcasted_iota(jnp.int32, (shape[0], 1), 0)
    owner = lax.axis_index("tf") ^ (row // (2 * bins))
    freq = K0 + owner * bins + (row % (2 * bins)) // 2
    phase = freq * lax.broadcasted_iota(jnp.int32, shape, 1)
    phase = (phase + (row % 2) * (length // 4)) % length
    turn = (phase + length // 8) // (length // 4)
    x = (phase - turn * (length // 4)).astype(f32) * (2.0 * math.pi / length)
    y = x * x
    even = 1.0 + y * (-1 / 2 + y * (1 / 24 + y * (-1 / 720 + y * (1 / 40320))))
    odd = x * (1.0 + y * (-1 / 6 + y * (1 / 120 + y * (-1 / 5040 + y * (1 / 362880)))))
    wave = jnp.where(turn % 2 == 0, even, -odd)
    wave = jnp.where((turn // 2) % 2 == 0, wave, -wave)
    table[...] = (wave * (1.0 / math.sqrt(length))).astype(bf16)
    to = lax.broadcasted_iota(jnp.int32, (16 * win, 16 * win), 0)
    at = lax.broadcasted_iota(jnp.int32, (1, 16 * win), 1)
    shuffle = (to == (at % 16) * win + at // 16).astype(f32).astype(bf16)
    load.wait()
    for w in range(win):
        x = samples[w]
        xf = x.astype(f32)
        power = jnp.mean(xf * xf, axis=0, keepdims=True)
        y = jnp.dot(table[...], x, preferred_element_type=f32)
        spec[w] = (y * lax.rsqrt(power + 1e-06)).astype(bf16)
    for grp in range(2 * F // 16):
        block = spec[:, 16 * grp : 16 * grp + 16, :].reshape(16 * win, spec.shape[-1])
        turned = jnp.dot(shuffle, block, preferred_element_type=f32).astype(bf16)
        for j in range(4):
            k, p = divmod(grp * 4 + j, bins // 2)
            outs[k][p] = turned[4 * win * j : 4 * win * (j + 1)]


def select_kernel(cols, *refs):
    slabs, out = refs[:-1], refs[-1]
    count, rows, chans = slabs[0].shape
    lanes = cols.shape[1]
    pick = (lax.broadcasted_iota(jnp.int32, (chans, lanes), 0) == cols[...]).astype(f32).astype(bf16)
    first = lax.broadcasted_iota(jnp.int32, (rows, lanes), 1) < lanes // 2
    for d, slab in enumerate(slabs):
        for p in range(count // 2):
            pair = [
                jnp.dot(slab[p + half * (count // 2)], pick, preferred_element_type=f32)
                for half in range(2)
            ]
            out[d, p] = jnp.where(first, *pair).astype(bf16)


def cross_kernel(cfg, coef, *refs):
    win, scale, n_slab, counts, owners = cfg
    pos = lax.axis_index("chan")
    blk = owners(pos)
    out, buf, sem = refs[-3:]
    slabs, rest = refs[:n_slab], refs[n_slab:-3]
    panels = []
    for near, far in counts:
        panels.append((rest[:near], rest[near : near + far]))
        rest = rest[near + far :]
    n_blk = len(panels)
    src = panels[0][0][0].shape[-1] // 2
    chans = slabs[0].shape[-1]
    tall = n_blk * src
    pairs = buf.shape[0]

    def copy_out(p, half, b):
        at = pl.ds(pl.multiple_of(blk[b] * src, src), src)
        return pltpu.make_async_copy(
            buf.at[p, half, :, :, :, pl.ds(b * src, src), :],
            out.at[pl.ds(2 * (p + half * pairs), 2), :, :, at, :],
            sem.at[p, half, b],
        )

    def pair(p, _):
        turned = [[], []]
        for group in panels:
            stack = []
            for part in group:
                for d in range(part[0].shape[0]):
                    value = part[0][d, p].astype(f32)
                    for other in part[1:]:
                        value = value + other[d, p].astype(f32)
                    stack.append(value)
            for j in range(2):
                rows = [v[2 * win * j : 2 * win * (j + 1)] for v in stack]
                turned[j].append(jnp.transpose(jnp.concatenate(rows, axis=0)))
        for half in range(2):
            values = [slab[p + half * pairs].astype(f32) for slab in slabs]
            for j in range(2):
                plain, swapped = [], []
                for v in values:
                    re = v[2 * win * j : 2 * win * j + win]
                    im = v[2 * win * j + win : 2 * win * (j + 1)]
                    plain += [re, im]
                    swapped += [im, -re]
                right = jnp.concatenate(
                    [jnp.concatenate(plain, axis=0), jnp.concatenate(swapped, axis=0)], axis=1
                ).astype(bf16)
                left = [
                    (t[src * half : src * (half + 1)] * coef[g : g + 1]).astype(bf16)
                    for g in range(G)
                    for t in turned[j]
                ]
                left = jnp.concatenate(left, axis=0)
                got = (jnp.dot(left, right, preferred_element_type=f32) * scale).astype(bf16)
                for g in range(G):
                    for o in range(2):
                        buf[p, half, j, g, o] = got[
                            g * tall : (g + 1) * tall, o * chans : (o + 1) * chans
                        ]
            for b in range(n_blk):
                copy_out(p, half, b).start()
        return 0

    lax.fori_loop(0, pairs, pair, 0, unroll=UNROLL if pairs % UNROLL == 0 else 1)
    for p in range(pairs):
        for half in range(2):
            for b in range(n_blk):
                copy_out(p, half, b).wait()


def cost(us):
    return pl.CostEstimate(flops=int(us * 1.1e9), bytes_accessed=int(us * 3e6), transcendentals=0)


def shards(samples, quality, substack, sources):
    win, length, chans = samples.shape
    n_tf = lax.axis_size("tf")
    n_chan = lax.axis_size("chan")
    me = lax.axis_index("tf")
    pos = lax.axis_index("chan")
    bins = F // n_tf
    src = sources.shape[0] // n_chan
    rows = 4 * win
    order = (me ^ jnp.arange(n_tf, dtype=jnp.int32)).astype(jnp.int32)
    vmem = pl.BlockSpec(memory_space=pltpu.VMEM)
    hbm = pl.BlockSpec(memory_space=pltpu.HBM)

    shapes = [jax.ShapeDtypeStruct((bins // 2, rows, chans), bf16)] * n_tf
    got = pl.pallas_call(
        lambda *refs: head_kernel((win, n_tf, bins), *refs),
        in_specs=[hbm],
        out_specs=[vmem] * len(shapes),
        out_shape=shapes,
        scratch_shapes=[
            pltpu.VMEM(samples.shape, bf16),
            pltpu.VMEM((2 * F, length), bf16),
            pltpu.VMEM((win, 2 * F, chans), bf16),
            pltpu.SemaphoreType.DMA,
        ],
        compiler_params=pltpu.CompilerParams(vmem_limit_bytes=50 * 1024 * 1024),
        cost_estimate=cost(5),
        name="head",
    )(samples)
    own, for_core = got[0], got[1]

    def across(value, k):
        return lax.ppermute(value, "tf", [(i, i ^ k) for i in range(n_tf)])

    core = across(for_core, 1)
    mine = lax.dynamic_slice_in_dim(sources, pos * src, src, 0) - pos * chans
    cols = jnp.concatenate([mine, mine])[None, :]

    def select(slabs):
        count = slabs[0].shape[0]
        return pl.pallas_call(
            select_kernel,
            in_specs=[vmem] * (1 + len(slabs)),
            out_specs=vmem,
            out_shape=jax.ShapeDtypeStruct((len(slabs), count // 2, rows, 2 * src), bf16),
            cost_estimate=cost(0.5),
            compiler_params=pltpu.CompilerParams(vmem_limit_bytes=12 * 1024 * 1024),
            name="select",
        )(cols, *slabs)

    def spread(panel):
        if n_chan == 4:
            two = lax.ppermute(panel, "chan", [(i, i ^ 2) for i in range(4)])
            one = lax.ppermute(panel, "chan", [(i, i ^ 1) for i in range(4)])
            later, one, two = lax.optimization_barrier((panel, one, two))
            end = lax.ppermute(two, "chan", [(2, 3), (1, 0)])
            mid = lax.ppermute(later, "chan", [(1, 2), (2, 1)])
            return [[panel], [one], [two], [mid, end]]
        return [[panel]] + [
            [lax.ppermute(panel, "chan", [(i, (i + k) % n_chan) for i in range(n_chan)])]
            for k in range(1, n_chan)
        ]

    coef = jnp.where(
        substack[None, :] == jnp.arange(G, dtype=jnp.int32)[:, None],
        (quality[None, :].astype(f32) + 1.0) / 4.0,
        0.0,
    ).reshape(G, n_tf, win)
    coef = jnp.take(jnp.concatenate([coef, coef], axis=2), order, axis=1)
    coef = coef.reshape(G, 2 * n_tf * win)
    scale = 1.0 / math.sqrt(win * n_tf)

    far = [across(value, k + 2) for k, value in enumerate(got[2:])]
    near = spread(select([own, core]))
    *far, _, _ = lax.optimization_barrier((*far, near[1][0], near[2][0]))
    away = spread(select(far))
    out_shape = jax.ShapeDtypeStruct((bins, G, 2, src * n_chan, chans), bf16)
    groups = [[0, 1, 2], [3]] if n_chan == 4 else [list(range(n_chan))]
    stacks = None
    for group in groups:
        args, counts = [own, core, *far], []
        for b in group:
            args += near[b] + away[b]
            counts.append((len(near[b]), len(away[b])))

        def owners(at, group=group):
            return [at ^ b if n_chan == 4 else lax.rem(at - b + n_chan, n_chan) for b in group]

        cfg = (win, scale, n_tf, counts, owners)
        first = stacks is None
        extra = [] if first else [stacks]

        def body(*refs, cfg=cfg, first=first):
            cross_kernel(cfg, *(refs if first else refs[:-4] + refs[-3:]))

        stacks = pl.pallas_call(
            body,
            in_specs=[vmem] * (1 + len(args)) + [hbm] * len(extra),
            out_specs=hbm,
            out_shape=out_shape,
            scratch_shapes=[
                pltpu.VMEM((bins // 4, 2, 2, G, 2, len(group) * src, chans), bf16),
                pltpu.SemaphoreType.DMA((bins // 4, 2, len(group))),
            ],
            input_output_aliases={} if first else {1 + len(args): 0},
            compiler_params=pltpu.CompilerParams(vmem_limit_bytes=20 * 1024 * 1024),
            cost_estimate=cost(1.5 + bins * len(group) * src / 1000),
            name="cross",
        )(coef, *args, *extra)
    return stacks


def solution(mesh):
    in_specs = (P(("day", "tf"), None, "chan"), P("day"), P("day"), P())
    out_specs = P("tf", "day", None, None, "chan")
    return jax.shard_map(shards, mesh=mesh, in_specs=in_specs, out_specs=out_specs, check_vma=False)
```

```python
import math

import jax
import jax.numpy as jnp
from jax import lax
from jax.experimental import pallas as pl
from jax.experimental.pallas import tpu as pltpu
from jax.sharding import PartitionSpec as P

F = 96
K0 = 8
G = 2
UNROLL = 3
f32 = jnp.float32
bf16 = jnp.bfloat16


def head_kernel(cfg, samples_hbm, *refs):
    win, n_tf, bins = cfg
    outs, (samples, table, spec, sem) = refs[:-4], refs[-4:]
    load = pltpu.make_async_copy(samples_hbm, samples, sem)
    load.start()
    shape = table.shape
    length = shape[1]
    row = lax.broadcasted_iota(jnp.int32, (shape[0], 1), 0)
    owner = lax.axis_index("tf") ^ (row // (2 * bins))
    freq = K0 + owner * bins + (row % (2 * bins)) // 2
    phase = freq * lax.broadcasted_iota(jnp.int32, shape, 1)
    phase = (phase + (row % 2) * (length // 4)) % length
    turn = (phase + length // 8) // (length // 4)
    x = (phase - turn * (length // 4)).astype(f32) * (2.0 * math.pi / length)
    y = x * x
    even = 1.0 + y * (-1 / 2 + y * (1 / 24 + y * (-1 / 720 + y * (1 / 40320))))
    odd = x * (1.0 + y * (-1 / 6 + y * (1 / 120 + y * (-1 / 5040 + y * (1 / 362880)))))
    wave = jnp.where(turn % 2 == 0, even, -odd)
    wave = jnp.where((turn // 2) % 2 == 0, wave, -wave)
    table[...] = (wave * (1.0 / math.sqrt(length))).astype(bf16)
    whole = win // 8 * 8
    shuffles = []
    for count in (whole, win - whole):
        to = lax.broadcasted_iota(jnp.int32, (16 * count, 16 * count), 0)
        at = lax.broadcasted_iota(jnp.int32, (1, 16 * count), 1)
        shuffles.append((to == (at % 16) * count + at // 16).astype(f32).astype(bf16))
    load.wait()
    for w in range(win):
        x = samples[w]
        xf = x.astype(f32)
        power = jnp.mean(xf * xf, axis=0, keepdims=True)
        y = jnp.dot(table[...], x, preferred_element_type=f32)
        spec[w] = (y * lax.rsqrt(power + 1e-06)).astype(bf16)
    for grp in range(2 * F // 16):
        turned = []
        for shuffle, first, last in zip(shuffles, (0, whole), (whole, win)):
            block = spec[first:last, 16 * grp : 16 * grp + 16, :]
            block = block.reshape(16 * (last - first), spec.shape[-1])
            turned.append(jnp.dot(shuffle, block, preferred_element_type=f32))
        for j in range(4):
            k, p = divmod(grp * 4 + j, bins // 2)
            parts = [t[t.shape[0] // 4 * j : t.shape[0] // 4 * (j + 1)] for t in turned]
            outs[k][p] = jnp.concatenate(parts, axis=0).astype(bf16)


def select_kernel(cols, *refs):
    slabs, out = refs[:-1], refs[-1]
    count, rows, chans = slabs[0].shape
    lanes = cols.shape[1]
    pick = (lax.broadcasted_iota(jnp.int32, (chans, lanes), 0) == cols[...]).astype(f32).astype(bf16)
    first = lax.broadcasted_iota(jnp.int32, (rows, lanes), 1) < lanes // 2
    for d, slab in enumerate(slabs):
        for p in range(count // 2):
            pair = [
                jnp.dot(slab[p + half * (count // 2)], pick, preferred_element_type=f32)
                for half in range(2)
            ]
            out[d, p] = jnp.where(first, *pair).astype(bf16)


def cross_kernel(cfg, coef, *refs):
    win, scale, n_slab, counts, owners = cfg
    pos = lax.axis_index("chan")
    blk = owners(pos)
    out, buf, sem = refs[-3:]
    slabs, rest = refs[:n_slab], refs[n_slab:-3]
    panels = []
    for near, far in counts:
        panels.append((rest[:near], rest[near : near + far]))
        rest = rest[near + far :]
    n_blk = len(panels)
    src = panels[0][0][0].shape[-1] // 2
    chans = slabs[0].shape[-1]
    tall = n_blk * src
    pairs = buf.shape[0]

    def copy_out(p, half, b):
        at = pl.ds(pl.multiple_of(blk[b] * src, src), src)
        return pltpu.make_async_copy(
            buf.at[p, half, :, :, :, pl.ds(b * src, src), :],
            out.at[pl.ds(2 * (p + half * pairs), 2), :, :, at, :],
            sem.at[p, half, b],
        )

    whole = win // 8 * 8

    def spans(j):
        return (2 * whole * j, 2 * whole), (4 * whole + 2 * (win - whole) * j, 2 * (win - whole))

    def pair(p, _):
        turned = [[], []]
        for group in panels:
            stack = []
            for part in group:
                for d in range(part[0].shape[0]):
                    value = part[0][d, p].astype(f32)
                    for other in part[1:]:
                        value = value + other[d, p].astype(f32)
                    stack.append(value)
            for j in range(2):
                rows = [v[a : a + n] for a, n in spans(j) for v in stack]
                turned[j].append(jnp.transpose(jnp.concatenate(rows, axis=0)))
        for half in range(2):
            values = [slab[p + half * pairs].astype(f32) for slab in slabs]
            for j in range(2):
                plain, swapped = [], []
                for a, n in spans(j):
                    for v in values:
                        re, im = v[a : a + n // 2], v[a + n // 2 : a + n]
                        plain += [re, im]
                        swapped += [im, -re]
                right = jnp.concatenate(
                    [jnp.concatenate(plain, axis=0), jnp.concatenate(swapped, axis=0)], axis=1
                ).astype(bf16)
                left = [
                    (t[src * half : src * (half + 1)] * coef[g : g + 1]).astype(bf16)
                    for g in range(G)
                    for t in turned[j]
                ]
                left = jnp.concatenate(left, axis=0)
                got = (jnp.dot(left, right, preferred_element_type=f32) * scale).astype(bf16)
                for g in range(G):
                    for o in range(2):
                        buf[p, half, j, g, o] = got[
                            g * tall : (g + 1) * tall, o * chans : (o + 1) * chans
                        ]
            for b in range(n_blk):
                copy_out(p, half, b).start()
        return 0

    lax.fori_loop(0, pairs, pair, 0, unroll=UNROLL if pairs % UNROLL == 0 else 1)
    for p in range(pairs):
        for half in range(2):
            for b in range(n_blk):
                copy_out(p, half, b).wait()


def cost(us):
    return pl.CostEstimate(flops=int(us * 1.1e9), bytes_accessed=int(us * 3e6), transcendentals=0)


def shards(samples, quality, substack, sources):
    win, length, chans = samples.shape
    n_tf = lax.axis_size("tf")
    n_chan = lax.axis_size("chan")
    me = lax.axis_index("tf")
    pos = lax.axis_index("chan")
    bins = F // n_tf
    src = sources.shape[0] // n_chan
    rows = 4 * win
    order = (me ^ jnp.arange(n_tf, dtype=jnp.int32)).astype(jnp.int32)
    vmem = pl.BlockSpec(memory_space=pltpu.VMEM)
    hbm = pl.BlockSpec(memory_space=pltpu.HBM)

    shapes = [jax.ShapeDtypeStruct((bins // 2, rows, chans), bf16)] * n_tf
    got = pl.pallas_call(
        lambda *refs: head_kernel((win, n_tf, bins), *refs),
        in_specs=[hbm],
        out_specs=[vmem] * len(shapes),
        out_shape=shapes,
        scratch_shapes=[
            pltpu.VMEM(samples.shape, bf16),
            pltpu.VMEM((2 * F, length), bf16),
            pltpu.VMEM((win, 2 * F, chans), bf16),
            pltpu.SemaphoreType.DMA,
        ],
        compiler_params=pltpu.CompilerParams(vmem_limit_bytes=50 * 1024 * 1024),
        cost_estimate=cost(5),
        name="head",
    )(samples)
    own, for_core = got[0], got[1]

    def across(value, k):
        return lax.ppermute(value, "tf", [(i, i ^ k) for i in range(n_tf)])

    core = across(for_core, 1)
    mine = lax.dynamic_slice_in_dim(sources, pos * src, src, 0) - pos * chans
    cols = jnp.concatenate([mine, mine])[None, :]

    def select(slabs):
        count = slabs[0].shape[0]
        return pl.pallas_call(
            select_kernel,
            in_specs=[vmem] * (1 + len(slabs)),
            out_specs=vmem,
            out_shape=jax.ShapeDtypeStruct((len(slabs), count // 2, rows, 2 * src), bf16),
            cost_estimate=cost(0.5),
            compiler_params=pltpu.CompilerParams(vmem_limit_bytes=12 * 1024 * 1024),
            name="select",
        )(cols, *slabs)

    def spread(panel):
        if n_chan == 4:
            two = lax.ppermute(panel, "chan", [(i, i ^ 2) for i in range(4)])
            one = lax.ppermute(panel, "chan", [(i, i ^ 1) for i in range(4)])
            later, one, two = lax.optimization_barrier((panel, one, two))
            mid = lax.ppermute(later, "chan", [(1, 2), (2, 1)])
            end = lax.ppermute(two, "chan", [(2, 3), (1, 0)])
            return [[panel], [one], [two], [end, mid]]
        return [[panel]] + [
            [lax.ppermute(panel, "chan", [(i, (i + k) % n_chan) for i in range(n_chan)])]
            for k in range(1, n_chan)
        ]

    coef = jnp.where(
        substack[None, :] == jnp.arange(G, dtype=jnp.int32)[:, None],
        (quality[None, :].astype(f32) + 1.0) / 4.0,
        0.0,
    ).reshape(G, n_tf, win)
    coef = jnp.take(coef, order, axis=1)
    halves = [coef[..., : win // 8 * 8], coef[..., win // 8 * 8 :]]
    halves = [jnp.concatenate([h, h], axis=2).reshape(G, -1) for h in halves]
    coef = jnp.concatenate(halves, axis=1)
    scale = 1.0 / math.sqrt(win * n_tf)

    far = [across(value, k + 2) for k, value in enumerate(got[2:])]
    near = spread(select([own, core]))
    *far, _, _ = lax.optimization_barrier((*far, near[1][0], near[2][0]))
    away = spread(select(far))
    out_shape = jax.ShapeDtypeStruct((bins, G, 2, src * n_chan, chans), bf16)
    groups = [[0], [1, 2], [3]] if n_chan == 4 else [list(range(n_chan))]
    stacks = None
    for group in groups:
        args, counts = [own, core, *far], []
        for b in group:
            args += near[b] + away[b]
            counts.append((len(near[b]), len(away[b])))

        def owners(at, group=group):
            return [at ^ b if n_chan == 4 else lax.rem(at - b + n_chan, n_chan) for b in group]

        cfg = (win, scale, n_tf, counts, owners)
        first = stacks is None
        extra = [] if first else [stacks]

        def body(*refs, cfg=cfg, first=first):
            cross_kernel(cfg, *(refs if first else refs[:-4] + refs[-3:]))

        stacks = pl.pallas_call(
            body,
            in_specs=[vmem] * (1 + len(args)) + [hbm] * len(extra),
            out_specs=hbm,
            out_shape=out_shape,
            scratch_shapes=[
                pltpu.VMEM((bins // 4, 2, 2, G, 2, len(group) * src, chans), bf16),
                pltpu.SemaphoreType.DMA((bins // 4, 2, len(group))),
            ],
            input_output_aliases={} if first else {1 + len(args): 0},
            compiler_params=pltpu.CompilerParams(vmem_limit_bytes=20 * 1024 * 1024),
            cost_estimate=cost(1.5 + bins * len(group) * src / 1000),
            name="cross",
        )(coef, *args, *extra)
    return stacks


def solution(mesh):
    in_specs = (P(("day", "tf"), None, "chan"), P("day"), P("day"), P())
    out_specs = P("tf", "day", None, None, "chan")
    return jax.shard_map(shards, mesh=mesh, in_specs=in_specs, out_specs=out_specs, check_vma=False)
```
